32 devices in a mesh: section: 2 (over core), rep: 4 (over z), fsdp: 4 (over y, x).
Axes of the slice: x: 2, y: 2, z: 4, core: 2. Of those that a mesh axis runs over, the one named last changes fastest.
Arguments:
- inputs: bfloat16 [2, 4, 1024, 576], P(None, 'rep', 'fsdp'), may hold values from -6 to 6
- cotangent: bfloat16 [2, 4, 1024, 576], P(None, 'rep', 'fsdp'), may hold values from -6 to 6
- segments: int32 [2, 4, 1024], P(None, 'rep'), may hold values from 0 to 17, as said below
- query_weight: bfloat16 [2, 576, 576], P('section', 'fsdp'), may hold values from -0.25 to 0.25
- key_weight: bfloat16 [2, 576, 192], P('section', 'fsdp'), may hold values from -0.25 to 0.25
- value_weight: bfloat16 [2, 576, 192], P('section', 'fsdp'), may hold values from -0.25 to 0.25
- output_weight: bfloat16 [2, 576, 576], P('section', 'fsdp'), may hold values from -1 to 1
- gate_weight: bfloat16 [2, 576, 1536], P('section', 'fsdp'), may hold values from -0.25 to 0.25
- up_weight: bfloat16 [2, 576, 1536], P('section', 'fsdp'), may hold values from -0.25 to 0.25
- down_weight: bfloat16 [2, 1536, 576], P('section', 'fsdp'), may hold values from -0.15625 to 0.15625
- attention_gain: bfloat16 [2, 576], P('section', 'fsdp'), may hold values from 0.25 to 1.75
- feedforward_gain: bfloat16 [2, 576], P('section', 'fsdp'), may hold values from 0.25 to 1.75
Outputs:
- section_output: bfloat16 [2, 2, 4, 1024, 576], P('section', None, 'rep', 'fsdp')
- input_grad: float32 [2, 2, 4, 1024, 576], P('section', None, 'rep', 'fsdp')
- query_grad: float32 [2, 576, 576], P('section', 'fsdp')
- key_grad: float32 [2, 576, 192], P('section', 'fsdp')
- value_grad: float32 [2, 576, 192], P('section', 'fsdp')
- output_grad: float32 [2, 576, 576], P('section', 'fsdp')
- gate_grad: float32 [2, 576, 1536], P('section', 'fsdp')
- up_grad: float32 [2, 576, 1536], P('section', 'fsdp')
- down_grad: float32 [2, 1536, 576], P('section', 'fsdp')
- attention_gain_grad: float32 [2, 576], P('section', 'fsdp')
- feedforward_gain_grad: float32 [2, 576], P('section', 'fsdp')
The draws below stay inside these ranges and needn't reach their ends.
Inputs may be any that keep to these rules, and one draw needn't show every extreme that they name: `segments`: segment numbers of a sequence start at 0 and never fall; each document of a sequence with several documents holds 60 to 800 tokens, but the last of a sequence may be shorter; for each sequence index, the sequence of one micro-batch is a single document; in each draw one sequence of another micro-batch is cut into documents of exactly 60 tokens (its last may be shorter).
All inputs are finite; a program needn't handle non-finite values.
Results may differ from the reference program's by a relative error of at most 0.025.
Values may be sent and summed in bfloat16 or wider, within the bound.
A program may use at most 192 MiB of HBM per device.

```python
import jax
import jax.numpy as jnp
from jax import lax

D = 576
FF = 1536
QH = 9
KVH = 3
HD = 64
QD = 576
KD = 192
MB = 2
LEN = 1024
SEQS = 4
DOC_MIN = 60
DOC_MAX = 800


def draw_segments(key, part):
    key = jax.random.fold_in(key, 11)
    length_key, whole_key, pick_key = jax.random.split(key, 3)
    pieces = LEN // DOC_MIN + 1
    spans = jax.random.randint(length_key, (MB, SEQS, pieces), DOC_MIN, DOC_MAX + 1, dtype=jnp.int32)
    single = jax.random.randint(whole_key, (SEQS,), 0, MB, dtype=jnp.int32)
    picked = jax.random.randint(pick_key, (), 0, SEQS, dtype=jnp.int32)
    other = (single[picked] + 1) % MB
    batch_ids = jnp.arange(MB, dtype=jnp.int32)[:, None, None]
    seq_ids = jnp.arange(SEQS, dtype=jnp.int32)[None, :, None]
    finest = (batch_ids == other) & (seq_ids == picked)
    spans = jnp.where(finest, jnp.full_like(spans, DOC_MIN), spans)
    bounds = jnp.cumsum(spans, axis=-1)
    places = jnp.arange(LEN, dtype=jnp.int32)
    numbers = jnp.sum((bounds[:, :, None, :] <= places[None, None, :, None]).astype(jnp.int32), axis=-1)
    chosen = jnp.arange(MB, dtype=jnp.int32)[:, None] == single[None, :]
    return jnp.where(chosen[:, :, None], jnp.zeros_like(numbers), numbers).astype(jnp.int32)


def block_levels(rng, extent, cuts, smallest, high):
    factor_of = 1.0
    for axis_at, blocks in cuts:
        heights = jax.random.uniform(jax.random.fold_in(jax.random.fold_in(rng, 6), axis_at), (blocks,), jnp.float32, smallest / len(cuts), high / len(cuts))
        factor_of = factor_of * jnp.repeat(jnp.exp(heights), extent[axis_at] // blocks).reshape((-1,) + (1,) * (len(extent) - 1 - axis_at))
    return factor_of


def scatter_about(own_key, dims, scale, bound, cuts=(), kind=jnp.bfloat16):
    level = block_levels(own_key, dims, cuts, -0.22, 0.18) if cuts else 1.0
    array = jax.random.normal(own_key, dims, jnp.float32) * scale * level
    return jnp.minimum(jnp.maximum(array, -bound), bound).astype(kind)


def setup_inputs(seed: int = 0) -> dict:
    streams_of = jax.random.split(jax.random.key(seed), 13)
    return {
        "inputs": scatter_about(streams_of[0], (MB, SEQS, LEN, D), 1.0, 6.0, ((1, 4), (2, 4))),
        "cotangent": scatter_about(streams_of[1], (MB, SEQS, LEN, D), 1.0, 6.0, ((1, 4), (2, 4))),
        "segments": draw_segments(jax.random.fold_in(streams_of[12], 71), 0),
        "query_weight": scatter_about(streams_of[3], (2, D, QD), D ** -0.5, 0.25, ((0, 2), (1, 4))),
        "key_weight": scatter_about(streams_of[4], (2, D, KD), D ** -0.5, 0.25, ((0, 2), (1, 4))),
        "value_weight": scatter_about(streams_of[5], (2, D, KD), D ** -0.5, 0.25, ((0, 2), (1, 4))),
        "output_weight": scatter_about(streams_of[6], (2, QD, D), (QD // 16) ** -0.5, 1.0, ((0, 2), (1, 4))),
        "gate_weight": scatter_about(streams_of[7], (2, D, FF), D ** -0.5, 0.25, ((0, 2), (1, 4))),
        "up_weight": scatter_about(streams_of[8], (2, D, FF), D ** -0.5, 0.25, ((0, 2), (1, 4))),
        "down_weight": scatter_about(streams_of[9], (2, FF, D), FF ** -0.5, 0.15625, ((0, 2), (1, 4))),
        "attention_gain": jnp.clip(1.0 + 0.15 * jax.random.normal(streams_of[10], (2, D), jnp.float32), 0.25, 1.75).astype(jnp.bfloat16),
        "feedforward_gain": jnp.clip(1.0 + 0.15 * jax.random.normal(streams_of[11], (2, D), jnp.float32), 0.25, 1.75).astype(jnp.bfloat16),
    }


@jax.custom_vjp
def low(v):
    return lax.optimization_barrier(v.astype(jnp.bfloat16)).astype(jnp.float32)

@jax.custom_vjp
def low_back(v):
    return v

def low_keep(v):
    return (low(v), None)

def low_pass(kept, grad):
    return (grad,)

def back_keep(v):
    return (v, None)

def back_low(kept, grad):
    return (low(grad),)
low.defvjp(low_keep, low_pass)
low_back.defvjp(back_keep, back_low)
EPS_NORM = 1e-05
ROPE_BASE = 100000.0

def product(left, right):
    return jnp.dot(left, right, precision=lax.Precision.HIGHEST, preferred_element_type=jnp.float32)

def norm_rows(values, gain):
    return values * lax.rsqrt(lax.optimization_barrier(jnp.mean(values * values, -1, keepdims=True)) + EPS_NORM) * gain

def doc_positions(segment_ids):
    places = jnp.arange(segment_ids.shape[0], dtype=jnp.int32)
    change = jnp.concatenate([jnp.ones((1,), jnp.bool_), segment_ids[1:] != segment_ids[:-1]])
    starts = jnp.where(change, places, jnp.zeros_like(places))
    firsts = lax.cummax(starts, axis=0)
    return (places - firsts).astype(jnp.float32)

def angle_table(positions, head_size):
    half = head_size // 2
    freqs = jnp.power(ROPE_BASE, -(jnp.arange(half, dtype=jnp.float32) * 2.0) / head_size)
    return positions[:, None] * freqs[None, :]

def rotary(tensor, angle):
    half = tensor.shape[-1] // 2
    cos_table = jnp.cos(angle)[:, None, :]
    sin_table = jnp.sin(angle)[:, None, :]
    front_half = tensor[..., :half]
    back_half = tensor[..., half:]
    return jnp.concatenate([front_half * cos_table - back_half * sin_table, back_half * cos_table + front_half * sin_table], -1)

def attention(queries, keys, values, allowed):
    group = QH // KVH
    scale = HD ** (-0.5)
    query_heads = jnp.transpose(queries, (1, 0, 2))
    key_heads = jnp.repeat(jnp.transpose(keys, (1, 0, 2)), group, axis=0)
    value_heads = jnp.repeat(jnp.transpose(values, (1, 0, 2)), group, axis=0)

    def one_head(item):
        query, key, value = item
        scores = low_back(product(query, key.T) * scale)
        scores = jnp.where(allowed, scores, -1e+30)
        raised = jnp.exp(scores - lax.optimization_barrier(jnp.max(scores, -1, keepdims=True)))
        weights = raised / lax.optimization_barrier(jnp.sum(raised, -1, keepdims=True))
        return product(low(weights), value)
    heads_out = lax.map(jax.checkpoint(one_head), (query_heads, key_heads, value_heads))
    return jnp.transpose(heads_out, (1, 0, 2)).reshape(queries.shape[0], QH * HD)

def layer(activation, params, section, segment_ids):
    query_weight, key_weight, value_weight, output_weight, gate_weight, up_weight, down_weight, attention_gain, feedforward_gain = [weight[section] for weight in params]
    length = activation.shape[0]
    angle = angle_table(doc_positions(segment_ids), HD)
    normed = low(norm_rows(activation, attention_gain))
    queries = low(rotary(low_back(product(normed, query_weight)).reshape(length, QH, HD), angle))
    keys = low(rotary(low_back(product(normed, key_weight)).reshape(length, KVH, HD), angle))
    values = low_back(low(product(normed, value_weight))).reshape(length, KVH, HD)
    places = jnp.arange(length, dtype=jnp.int32)
    allowed = (segment_ids[:, None] == segment_ids[None, :]) & (places[:, None] >= places[None, :])
    attended = low_back(low(attention(queries, keys, values, allowed)))
    middle = activation + low_back(product(attended, output_weight))
    normed_mid = low(norm_rows(middle, feedforward_gain))
    gate_pre = low_back(product(normed_mid, gate_weight))
    lifted = low_back(product(normed_mid, up_weight))
    hidden = low(jax.nn.silu(gate_pre) * lifted)
    return middle + low_back(product(hidden, down_weight))

def forward(first_input, probe, params, segment_ids):

    def one_sequence(carry, item):
        sequence, probe_rows, seq_ids = item
        handed = low(layer(sequence, params, 0, seq_ids))
        result = layer(low_back(handed + probe_rows), params, 1, seq_ids)
        return (carry, (handed, result))
    _, outputs = lax.scan(one_sequence, jnp.zeros((), jnp.float32), (first_input, probe, segment_ids))
    return outputs

def reference(inputs, cotangent, segments, query_weight, key_weight, value_weight, output_weight, gate_weight, up_weight, down_weight, attention_gain, feedforward_gain):
    batches, sequences, length, width = inputs.shape
    first_input = inputs.reshape(batches * sequences, length, width).astype(jnp.float32)
    segment_ids = segments.reshape(batches * sequences, length).astype(jnp.int32)
    params = tuple((weight.astype(jnp.float32) for weight in (query_weight, key_weight, value_weight, output_weight, gate_weight, up_weight, down_weight, attention_gain, feedforward_gain)))
    probe = jnp.zeros_like(first_input)
    outputs, pull = jax.vjp(lambda left, middle, right: forward(left, middle, right, segment_ids), first_input, probe, params)
    handed, result = outputs
    upstream = cotangent.reshape(batches * sequences, length, width).astype(jnp.float32)
    input_part, probe_part, grads = pull((jnp.zeros_like(handed), upstream))
    section_output = jnp.stack([handed, result]).reshape(2, batches, sequences, length, width).astype(jnp.bfloat16)
    input_grad = jnp.stack([input_part, probe_part]).reshape(2, batches, sequences, length, width)
    return (section_output, input_grad, grads[0], grads[1], grads[2], grads[3], grads[4], grads[5], grads[6], grads[7], grads[8])
```

```python
import functools

import jax
import jax.numpy as jnp
from jax import lax
from jax.experimental import pallas as pl
from jax.experimental.pallas import tpu as pltpu
from jax.sharding import PartitionSpec as P

QH = 9
KVH = 3
HD = 64
QD = QH * HD
KD = KVH * HD
GROUP = QH // KVH
EPS_NORM = 1e-05
ROPE_BASE = 100000.0
F32 = jnp.float32
BF16 = jnp.bfloat16


def dot(left, right, dims):
    return lax.dot_general(left, right, ((dims[:1], dims[1:]), ((), ())), preferred_element_type=F32)


def exchange(block, axis, distance):
    size = lax.axis_size(axis)
    return lax.ppermute(block, axis, [(i, i ^ distance) for i in range(size)])


def norm_rows(values, gain):
    return values * lax.rsqrt(jnp.mean(values * values, -1, keepdims=True) + EPS_NORM) * gain


def norm_back(values, gain, grad):
    scale = lax.rsqrt(jnp.mean(values * values, -1, keepdims=True) + EPS_NORM)
    unit = values * scale
    pulled = grad * gain
    back = scale * (pulled - unit * jnp.mean(pulled * unit, -1, keepdims=True))
    return back, jnp.sum(grad * unit, 0)


def rope(heads, cos, sin):
    half = HD // 2
    front, back = heads[:, :half], heads[:, half:]
    return jnp.concatenate([front * cos - back * sin, back * cos + front * sin], 1)


def allowed_keys(start_ref, pos_ref, kpos_ref):
    kpos = kpos_ref[...]
    return (kpos >= start_ref[...]) & (kpos <= pos_ref[...])


def attend_kernel(q_ref, k_ref, v_ref, start_ref, pos_ref, kpos_ref, o_ref, lse_ref):
    scores = dot(k_ref[0], q_ref[0], (0, 0))
    scores = jnp.where(allowed_keys(start_ref, pos_ref, kpos_ref), scores, -1e30)
    highest = jnp.max(scores, 0, keepdims=True)
    raised = jnp.exp(scores - highest)
    totals = jnp.sum(raised, 0, keepdims=True)
    weights = (raised * (1.0 / totals)).astype(BF16)
    o_ref[0] = dot(v_ref[0], weights, (1, 0)).astype(BF16)
    lse_ref[0] = highest + jnp.log(totals)


def attend_back_kernel(
    q_ref, k_ref, v_ref, start_ref, pos_ref, kpos_ref, lse_ref, do_ref, dq_ref, dk_ref, dv_ref
):
    query, key, grad_out = q_ref[0], k_ref[0], do_ref[0]
    scores = dot(key, query, (0, 0))
    scores = jnp.where(allowed_keys(start_ref, pos_ref, kpos_ref), scores, -1e30)
    weights = jnp.exp(scores - lse_ref[0])
    grad_weights = dot(v_ref[0], grad_out, (0, 0))
    row = jnp.sum(weights * grad_weights, 0, keepdims=True)
    grad_scores = (weights * (grad_weights - row)).astype(BF16)
    dq_ref[0] = dot(key, grad_scores, (1, 0)) * (HD**-0.5)
    grad_key = dot(query, grad_scores, (1, 1))
    grad_value = dot(grad_out, weights.astype(BF16), (1, 1))
    first = pl.program_id(0) % GROUP == 0

    @pl.when(first)
    def _():
        dk_ref[0] = grad_key
        dv_ref[0] = grad_value

    @pl.when(jnp.logical_not(first))
    def _():
        dk_ref[0] += grad_key
        dv_ref[0] += grad_value


def head_spec(rows, columns, index):
    return pl.BlockSpec((1, rows, columns), index)


def whole_spec(array):
    return pl.BlockSpec(array.shape, lambda h: (0,) * array.ndim)


def attention_specs(queries, keys_values, marks):
    rows, length = queries.shape[2], keys_values.shape[2]
    return [
        head_spec(HD, rows, lambda h: (h, 0, 0)),
        head_spec(HD, length, lambda h: (h // GROUP, 0, 0)),
        head_spec(HD, length, lambda h: (KVH + h // GROUP, 0, 0)),
    ] + [whole_spec(mark) for mark in marks]


PARAMS = pltpu.CompilerParams(vmem_limit_bytes=48 * 1024 * 1024)


def attend(queries, keys_values, marks):
    rows, length = queries.shape[2], keys_values.shape[2]
    return pl.pallas_call(
        attend_kernel,
        grid=(QH,),
        in_specs=attention_specs(queries, keys_values, marks),
        out_specs=[
            head_spec(HD, rows, lambda h: (h, 0, 0)),
            head_spec(1, rows, lambda h: (h, 0, 0)),
        ],
        out_shape=[
            jax.ShapeDtypeStruct((QH, HD, rows), BF16),
            jax.ShapeDtypeStruct((QH, 1, rows), F32),
        ],
        compiler_params=PARAMS,
        cost_estimate=pl.CostEstimate(
            flops=4 * QD * rows * length, bytes_accessed=2 * 2**20, transcendentals=QH * rows * length
        ),
        name="attend",
    )(queries, keys_values, keys_values, *marks)


def attend_back(queries, keys_values, marks, lse, grad_out):
    rows, length = queries.shape[2], keys_values.shape[2]
    return pl.pallas_call(
        attend_back_kernel,
        grid=(QH,),
        in_specs=attention_specs(queries, keys_values, marks)
        + [
            head_spec(1, rows, lambda h: (h, 0, 0)),
            head_spec(HD, rows, lambda h: (h, 0, 0)),
        ],
        out_specs=[
            head_spec(HD, rows, lambda h: (h, 0, 0)),
            head_spec(HD, length, lambda h: (h // GROUP, 0, 0)),
            head_spec(HD, length, lambda h: (h // GROUP, 0, 0)),
        ],
        out_shape=[
            jax.ShapeDtypeStruct((QH, HD, rows), F32),
            jax.ShapeDtypeStruct((KVH, HD, length), F32),
            jax.ShapeDtypeStruct((KVH, HD, length), F32),
        ],
        compiler_params=PARAMS,
        cost_estimate=pl.CostEstimate(
            flops=10 * QD * rows * length, bytes_accessed=4 * 2**20, transcendentals=QH * rows * length
        ),
        name="attend_back",
    )(queries, keys_values, keys_values, *marks, lse, grad_out)


def layer_forward(activation, weights, gains, cos, sin, marks):
    qkv_weight, output_weight, gate_up, down_weight = weights
    rows = activation.shape[0]
    fsdp = lax.axis_size("fsdp")
    normed = norm_rows(activation, gains[0]).astype(BF16)
    heads = dot(qkv_weight, normed, (0, 1)).reshape(QH + 2 * KVH, HD, rows)
    queries = (rope(heads[:QH], cos, sin).astype(BF16) * (HD**-0.5)).astype(BF16)
    mine = jnp.concatenate(
        [rope(heads[QH : QH + KVH], cos, sin).astype(BF16), heads[QH + KVH :].astype(BF16)], 0
    )
    keys_values = jnp.concatenate(
        [mine] + [exchange(mine, "fsdp", d) for d in range(1, fsdp)], 2
    )
    attended, lse = attend(queries, keys_values, marks)
    attended = attended.reshape(QD, rows)
    middle = activation + dot(attended, output_weight, (0, 0))
    normed_mid = norm_rows(middle, gains[1]).astype(BF16)
    both = dot(normed_mid, gate_up, (1, 0))
    half = both.shape[1] // 2
    gate, lift = both[:, :half], both[:, half:]
    hidden = (gate * jax.nn.sigmoid(gate) * lift).astype(BF16)
    result = middle + dot(hidden, down_weight, (1, 0))
    kept = (activation, normed, queries, keys_values, lse, attended, middle, normed_mid, both, hidden)
    return result, kept


def layer_backward(grad, kept, weights, gains, cos, sin, marks):
    qkv_weight, output_weight, gate_up, down_weight = weights
    activation, normed, queries, keys_values, lse, attended, middle, normed_mid, both, hidden = kept
    rows = activation.shape[0]
    fsdp = lax.axis_size("fsdp")
    half = both.shape[1] // 2
    gate, lift = both[:, :half], both[:, half:]
    branch = grad.astype(BF16)
    down_grad = dot(hidden, branch, (0, 0)).astype(BF16)
    hidden_grad = dot(branch, down_weight, (1, 1))
    sigma = jax.nn.sigmoid(gate)
    both_grad = jnp.concatenate(
        [
            (hidden_grad * lift * sigma * (1.0 + gate * (1.0 - sigma))).astype(BF16),
            (hidden_grad * gate * sigma).astype(BF16),
        ],
        1,
    )
    gate_up_grad = dot(normed_mid, both_grad, (0, 0)).astype(BF16)
    back, feedforward_gain_grad = norm_back(middle, gains[1], dot(both_grad, gate_up, (1, 1)))
    middle_grad = grad + back
    mid_branch = middle_grad.astype(BF16)
    output_grad = dot(attended, mid_branch, (1, 0)).astype(BF16)
    heads_grad = dot(output_weight, mid_branch, (1, 1)).astype(BF16).reshape(QH, HD, rows)
    dq, dk, dv = attend_back(queries, keys_values, marks, lse, heads_grad)
    parts = jnp.concatenate([dk, dv], 0).astype(BF16)
    pieces = [parts[:, :, d * rows : (d + 1) * rows] for d in range(fsdp)]
    summed = pieces[0].astype(F32)
    for d in range(1, fsdp):
        summed = summed + exchange(pieces[d], "fsdp", d).astype(F32)
    turned = rope(jnp.concatenate([dq, summed[:KVH]], 0), cos, -sin)
    raw = jnp.concatenate([turned, summed[KVH:]], 0).astype(BF16).reshape(QD + 2 * KD, rows)
    qkv_grad = dot(normed, raw, (0, 1)).astype(BF16)
    normed_grad = dot(raw, qkv_weight, (0, 1))
    back, attention_gain_grad = norm_back(activation, gains[0], normed_grad)
    return (
        middle_grad + back,
        (qkv_grad, output_grad, gate_up_grad, down_grad),
        jnp.stack([attention_gain_grad, feedforward_gain_grad]),
    )


def reduce_grads(grads, on_first):
    qkv_grad, output_grad, gate_up_grad, down_grad = grads
    fsdp, rep = lax.axis_size("fsdp"), lax.axis_size("rep")
    rows = qkv_grad.shape[0] // fsdp
    wide = gate_up_grad.shape[1]
    rest = jnp.concatenate(
        [qkv_grad, output_grad, down_grad.reshape(rows * fsdp, wide // 2)], 1
    )
    mine = jnp.where(on_first, gate_up_grad, rest)
    other = exchange(jnp.where(on_first, rest, gate_up_grad), "section", 1)
    total = (mine.astype(F32) + other.astype(F32)).astype(BF16)
    total = jnp.transpose(total.reshape(fsdp, rows, rep, wide // rep), (0, 2, 1, 3))
    for axis, size in (("fsdp", fsdp), ("rep", rep)):
        me = lax.axis_index(axis)
        own = lax.dynamic_index_in_dim(total, me, 0, keepdims=False).astype(F32)
        for d in range(1, size):
            piece = lax.dynamic_index_in_dim(total, me ^ d, 0, keepdims=False)
            own = own + exchange(piece, axis, d).astype(F32)
        total = own.astype(BF16)
    return lax.all_gather(total, "rep", axis=1, tiled=True)


def body(inputs, cotangent, segments, *shards):
    query, key, value, output, gate, up, down = [shard[0] for shard in shards[:7]]
    section = lax.axis_index("section")
    on_first = section == 0
    fsdp = lax.axis_size("fsdp")
    me = lax.axis_index("fsdp")
    rows, width = inputs.shape[2], inputs.shape[3]
    depth, wide = gate.shape[0], 2 * gate.shape[1]

    first_part = jnp.concatenate([gate, up], 1)
    second_part = jnp.concatenate([query, key, value, output, down.reshape(depth, wide // 2)], 1)
    swapped = exchange(jnp.where(on_first, second_part, first_part), "section", 1)
    shares = (
        jnp.where(on_first, first_part, swapped),
        jnp.where(on_first, swapped, second_part),
    )
    gain_shard = jnp.concatenate(shards[7:9], 0)
    gains = lax.all_gather(gain_shard, ("section", "fsdp"), axis=0)
    gains = jnp.transpose(gains.reshape(2, fsdp, 2, depth), (0, 2, 1, 3))
    gains = gains.reshape(2, 2, width).astype(F32)
    weights = []
    for share in shares:
        full = lax.all_gather(share, "fsdp", axis=0, tiled=True)
        other = exchange(full, "section", 1)
        gate_up = jnp.where(on_first, full, other)
        rest = jnp.where(on_first, other, full)
        qkv = QD + 2 * KD
        weights.append(
            (
                rest[:, :qkv],
                rest[:, qkv : qkv + width],
                gate_up,
                rest[:, qkv + width :].reshape(-1, width),
            )
        )

    segment_ids = lax.dynamic_index_in_dim(segments[:, 0], section, 0, keepdims=False)
    activation = lax.dynamic_index_in_dim(inputs[:, 0], section, 0, keepdims=False).astype(F32)
    upstream = lax.dynamic_index_in_dim(cotangent[:, 0], section, 0, keepdims=False).astype(F32)
    own_ids = lax.dynamic_slice_in_dim(segment_ids, me * rows, rows, 0)
    start = jnp.sum((segment_ids[:, None] < own_ids[None, :]).astype(jnp.int32), 0)
    places = jnp.arange(rows, dtype=jnp.int32)
    pos = me * rows + places
    key_pos = jnp.concatenate([(me ^ d) * rows + places for d in range(fsdp)])
    marks = (start[None, :], pos[None, :], key_pos[:, None])
    freqs = jnp.power(ROPE_BASE, -(jnp.arange(HD // 2, dtype=F32) * 2.0) / HD)
    angle = freqs[:, None] * (pos - start).astype(F32)[None, :]
    cos, sin = jnp.cos(angle), jnp.sin(angle)

    result, kept0 = layer_forward(activation, weights[0], gains[0], cos, sin, marks)
    handed = result.astype(BF16)
    result, kept1 = layer_forward(handed.astype(F32), weights[1], gains[1], cos, sin, marks)
    final = result.astype(BF16)

    def sorted_out(first, second, send_first, send_second):
        received = exchange(jnp.where(on_first, send_second, send_first), "section", 1)
        received = received.astype(first.dtype)
        both = [jnp.where(on_first, first, received), jnp.where(on_first, received, second)]
        return jnp.stack(both)[None, :, None]

    section_output = sorted_out(handed, final, handed, final)
    grad, grads1, gain_grads1 = layer_backward(
        upstream, kept1, weights[1], gains[1], cos, sin, marks
    )
    part1 = reduce_grads(grads1, on_first)
    returned = grad.astype(BF16)
    grad, grads0, gain_grads0 = layer_backward(
        returned.astype(F32), kept0, weights[0], gains[0], cos, sin, marks
    )
    part0 = reduce_grads(grads0, on_first)
    input_grad = sorted_out(grad, returned.astype(F32), grad.astype(BF16), returned)

    other = exchange(jnp.where(on_first, part1, part0), "section", 1)
    gate_up_grad = jnp.where(on_first, part0, other).astype(F32)
    rest = jnp.where(on_first, other, part1).astype(F32)
    gain_grads = lax.psum(
        jnp.stack([gain_grads0, gain_grads1]), ("section", "rep", "fsdp")
    )
    gain_grads = lax.dynamic_index_in_dim(gain_grads, section, 0, keepdims=False)
    gain_grads = lax.dynamic_slice_in_dim(gain_grads, me * depth, depth, 1)
    half = wide // 2
    return (
        section_output,
        input_grad,
        rest[None, :, :QD],
        rest[None, :, QD : QD + KD],
        rest[None, :, QD + KD : QD + 2 * KD],
        rest[None, :, QD + 2 * KD : half],
        gate_up_grad[None, :, :half],
        gate_up_grad[None, :, half:],
        rest[:, half:].reshape(1, -1, width),
        gain_grads[:1],
        gain_grads[1:],
    )


def solution(mesh):
    rows = P("section", "fsdp", None)
    tokens = P("section", None, "rep", "fsdp", None)
    vector = P("section", "fsdp")
    return jax.shard_map(
        body,
        mesh=mesh,
        in_specs=(P(None, "rep", "fsdp", None),) * 2
        + (P(None, "rep", None),)
        + (rows,) * 7
        + (vector,) * 2,
        out_specs=(tokens,) * 2 + (rows,) * 7 + (vector,) * 2,
        check_vma=False,
    )
```

```python
import jax
import jax.numpy as jnp
from jax import lax
from jax.experimental import pallas as pl
from jax.experimental.pallas import tpu as pltpu
from jax.sharding import PartitionSpec as P

QH = 9
KVH = 3
HD = 64
QD = QH * HD
KD = KVH * HD
GROUP = QH // KVH
EPS_NORM = 1e-05
ROPE_BASE = 100000.0
F32 = jnp.float32
BF16 = jnp.bfloat16


def dot(left, right, dims):
    return lax.dot_general(left, right, ((dims[:1], dims[1:]), ((), ())), preferred_element_type=F32)


def exchange(block, axis, distance):
    size = lax.axis_size(axis)
    return lax.ppermute(block, axis, [(i, i ^ distance) for i in range(size)])


def norm_rows(values, gain):
    return values * lax.rsqrt(jnp.mean(values * values, -1, keepdims=True) + EPS_NORM) * gain


def norm_back(values, gain, grad):
    scale = lax.rsqrt(jnp.mean(values * values, -1, keepdims=True) + EPS_NORM)
    unit = values * scale
    pulled = grad * gain
    back = scale * (pulled - unit * jnp.mean(pulled * unit, -1, keepdims=True))
    return back, jnp.sum(grad * unit, 0)


def rope(heads, cos, sin):
    half = HD // 2
    front, back = heads[:, :half], heads[:, half:]
    return jnp.concatenate([front * cos - back * sin, back * cos + front * sin], 1)


def allowed_keys(start_ref, pos_ref, kpos_ref):
    kpos = kpos_ref[...]
    return (kpos >= start_ref[...]) & (kpos <= pos_ref[...])


def attend_kernel(q_ref, k_ref, v_ref, start_ref, pos_ref, kpos_ref, o_ref, lse_ref):
    scores = dot(k_ref[0], q_ref[0], (0, 0))
    scores = jnp.where(allowed_keys(start_ref, pos_ref, kpos_ref), scores, -1e30)
    highest = jnp.max(scores, 0, keepdims=True)
    raised = jnp.exp(scores - highest)
    totals = jnp.sum(raised, 0, keepdims=True)
    weights = (raised * (1.0 / totals)).astype(BF16)
    o_ref[0] = dot(v_ref[0], weights, (1, 0)).astype(BF16)
    lse_ref[0] = highest + jnp.log(totals)


def attend_back_kernel(
    q_ref, k_ref, v_ref, start_ref, pos_ref, kpos_ref, lse_ref, do_ref, dq_ref, dk_ref, dv_ref
):
    query, key, grad_out = q_ref[0], k_ref[0], do_ref[0]
    scores = dot(key, query, (0, 0))
    scores = jnp.where(allowed_keys(start_ref, pos_ref, kpos_ref), scores, -1e30)
    weights = jnp.exp(scores - lse_ref[0])
    grad_weights = dot(v_ref[0], grad_out, (0, 0))
    row = jnp.sum(weights * grad_weights, 0, keepdims=True)
    grad_scores = (weights * (grad_weights - row)).astype(BF16)
    dq_ref[0] = dot(key, grad_scores, (1, 0)) * (HD**-0.5)
    grad_key = dot(query, grad_scores, (1, 1))
    grad_value = dot(grad_out, weights.astype(BF16), (1, 1))
    first = pl.program_id(0) % GROUP == 0

    @pl.when(first)
    def _():
        dk_ref[0] = grad_key
        dv_ref[0] = grad_value

    @pl.when(jnp.logical_not(first))
    def _():
        dk_ref[0] += grad_key
        dv_ref[0] += grad_value


def head_spec(rows, columns, index):
    return pl.BlockSpec((1, rows, columns), index)


def whole_spec(array):
    return pl.BlockSpec(array.shape, lambda h: (0,) * array.ndim)


def attention_specs(queries, keys_values, marks):
    rows, length = queries.shape[2], keys_values.shape[2]
    return [
        head_spec(HD, rows, lambda h: (h, 0, 0)),
        head_spec(HD, length, lambda h: (h // GROUP, 0, 0)),
        head_spec(HD, length, lambda h: (KVH + h // GROUP, 0, 0)),
    ] + [whole_spec(mark) for mark in marks]


PARAMS = pltpu.CompilerParams(vmem_limit_bytes=48 * 1024 * 1024)


def attend(queries, keys_values, marks):
    rows, length = queries.shape[2], keys_values.shape[2]
    return pl.pallas_call(
        attend_kernel,
        grid=(QH,),
        in_specs=attention_specs(queries, keys_values, marks),
        out_specs=[
            head_spec(HD, rows, lambda h: (h, 0, 0)),
            head_spec(1, rows, lambda h: (h, 0, 0)),
        ],
        out_shape=[
            jax.ShapeDtypeStruct((QH, HD, rows), BF16),
            jax.ShapeDtypeStruct((QH, 1, rows), F32),
        ],
        compiler_params=PARAMS,
        cost_estimate=pl.CostEstimate(
            flops=4 * QD * rows * length, bytes_accessed=2 * 2**20, transcendentals=QH * rows * length
        ),
        name="attend",
    )(queries, keys_values, keys_values, *marks)


def attend_back(queries, keys_values, marks, lse, grad_out):
    rows, length = queries.shape[2], keys_values.shape[2]
    return pl.pallas_call(
        attend_back_kernel,
        grid=(QH,),
        in_specs=attention_specs(queries, keys_values, marks)
        + [
            head_spec(1, rows, lambda h: (h, 0, 0)),
            head_spec(HD, rows, lambda h: (h, 0, 0)),
        ],
        out_specs=[
            head_spec(HD, rows, lambda h: (h, 0, 0)),
            head_spec(HD, length, lambda h: (h // GROUP, 0, 0)),
            head_spec(HD, length, lambda h: (h // GROUP, 0, 0)),
        ],
        out_shape=[
            jax.ShapeDtypeStruct((QH, HD, rows), F32),
            jax.ShapeDtypeStruct((KVH, HD, length), F32),
            jax.ShapeDtypeStruct((KVH, HD, length), F32),
        ],
        compiler_params=PARAMS,
        cost_estimate=pl.CostEstimate(
            flops=10 * QD * rows * length, bytes_accessed=4 * 2**20, transcendentals=QH * rows * length
        ),
        name="attend_back",
    )(queries, keys_values, keys_values, *marks, lse, grad_out)


def layer_forward(activation, weights, gains, cos, sin, marks):
    qkv_weight, output_weight, gate_up, down_weight = weights
    rows = activation.shape[0]
    fsdp = lax.axis_size("fsdp")
    normed = norm_rows(activation, gains[0]).astype(BF16)
    heads = dot(qkv_weight, normed, (0, 1)).reshape(QH + 2 * KVH, HD, rows)
    queries = (rope(heads[:QH], cos, sin).astype(BF16) * (HD**-0.5)).astype(BF16)
    mine = jnp.concatenate(
        [rope(heads[QH : QH + KVH], cos, sin).astype(BF16), heads[QH + KVH :].astype(BF16)], 0
    )
    keys_values = jnp.concatenate(
        [mine] + [exchange(mine, "fsdp", d) for d in range(1, fsdp)], 2
    )
    attended, lse = attend(queries, keys_values, marks)
    attended = attended.reshape(QD, rows)
    middle = activation + dot(attended, output_weight, (0, 0))
    normed_mid = norm_rows(middle, gains[1]).astype(BF16)
    gate, lift = [dot(normed_mid, weight, (1, 0)) for weight in gate_up]
    hidden = (gate * jax.nn.sigmoid(gate) * lift).astype(BF16)
    result = middle + dot(hidden, down_weight, (1, 0))
    kept = (activation, normed, queries, keys_values, lse, attended, middle, normed_mid, gate, lift, hidden)
    return result, kept


def feedforward_back(grad, kept, weights, gains):
    _, _, gate_up, down_weight = weights
    middle, normed_mid, gate, lift, hidden = kept[6:]
    branch = grad.astype(BF16)
    down_grad = dot(hidden, branch, (0, 0)).astype(BF16)
    hidden_grad = dot(branch, down_weight, (1, 1))
    sigma = jax.nn.sigmoid(gate)
    gate_part = (hidden_grad * lift * sigma * (1.0 + gate * (1.0 - sigma))).astype(BF16)
    lift_part = (hidden_grad * gate * sigma).astype(BF16)
    gate_grad = dot(normed_mid, gate_part, (0, 0)).astype(BF16)
    up_grad = dot(normed_mid, lift_part, (0, 0)).astype(BF16)
    pulled = dot(gate_part, gate_up[0], (1, 1)) + dot(lift_part, gate_up[1], (1, 1))
    back, gain_grad = norm_back(middle, gains[1], pulled)
    return grad + back, gate_grad, up_grad, down_grad, gain_grad


def projections_back(middle_grad, dq, dk, dv, kept, weights, gains, cos, sin):
    activation, normed = kept[:2]
    qkv_weight = weights[0]
    rows = activation.shape[0]
    fsdp = lax.axis_size("fsdp")
    parts = jnp.concatenate([dk, dv], 0).astype(BF16)
    pieces = [parts[:, :, d * rows : (d + 1) * rows] for d in range(fsdp)]
    summed = pieces[0].astype(F32)
    for d in range(1, fsdp):
        summed = summed + exchange(pieces[d], "fsdp", d).astype(F32)
    turned = rope(jnp.concatenate([dq, summed[:KVH]], 0), cos, -sin)
    raw = jnp.concatenate([turned, summed[KVH:]], 0).astype(BF16).reshape(QD + 2 * KD, rows)
    qkv_grad = dot(normed, raw, (0, 1)).astype(BF16)
    back, gain_grad = norm_back(activation, gains[0], dot(raw, qkv_weight, (0, 1)))
    return middle_grad + back, qkv_grad, gain_grad


def sum_section(left, right, on_first):
    other = exchange(jnp.where(on_first, right, left), "section", 1)
    return (jnp.where(on_first, left, right).astype(F32) + other.astype(F32)).astype(BF16)


def sum_scatter(total, axis, dim):
    size, me = lax.axis_size(axis), lax.axis_index(axis)
    span = total.shape[dim] // size
    own = lax.dynamic_slice_in_dim(total, me * span, span, dim).astype(F32)
    for d in range(1, size):
        piece = lax.dynamic_slice_in_dim(total, (me ^ d) * span, span, dim)
        own = own + exchange(piece, axis, d).astype(F32)
    return own.astype(BF16)


def collect(share, axis, dim):
    size, me = lax.axis_size(axis), lax.axis_index(axis)
    span = share.shape[dim]
    shape = list(share.shape)
    shape[dim] = span * size
    full = jnp.zeros(shape, share.dtype)
    for d in range(size):
        block = share if d == 0 else exchange(share, axis, d)
        full = lax.dynamic_update_slice_in_dim(full, block, (me ^ d) * span, dim)
    return full


def tie(*arrays):
    return lax.optimization_barrier(arrays)


def body(inputs, cotangent, segments, *shards):
    query, key, value, output, gate, up, down = [shard[0] for shard in shards[:7]]
    section = lax.axis_index("section")
    on_first = section == 0
    fsdp, rep = lax.axis_size("fsdp"), lax.axis_size("rep")
    me = lax.axis_index("fsdp")
    rows, width = inputs.shape[2], inputs.shape[3]
    depth, half = gate.shape
    qkv = QD + 2 * KD

    attention_shard = jnp.concatenate([query, key, value, output], 1)
    down_shard = down.reshape(depth, half)
    shares = []
    for left, right in ((attention_shard, down_shard), (gate, up)):
        swapped = exchange(jnp.where(on_first, right, left), "section", 1)
        shares.append(
            (jnp.where(on_first, left, swapped), jnp.where(on_first, swapped, right))
        )
    gain_shard = jnp.concatenate(shards[7:9], 0)
    other = exchange(gain_shard, "section", 1)
    gain_shard = jnp.stack(
        [jnp.where(on_first, gain_shard, other), jnp.where(on_first, other, gain_shard)]
    )
    gains = collect(gain_shard[None], "fsdp", 0)
    gains = jnp.transpose(gains, (1, 2, 0, 3)).reshape(2, 2, width).astype(F32)

    def both_parts(full):
        other = exchange(full, "section", 1)
        return jnp.where(on_first, full, other), jnp.where(on_first, other, full)

    weights = []
    before = None
    for layer in range(2):
        pairs = []
        for kind in range(2):
            share = shares[kind][layer]
            if before is not None:
                share, before = tie(share, before)
                if kind == 1:
                    pairs[0] = before
                elif layer == 1:
                    weights[0][1] = before
            before = collect(share, "fsdp", 0)
            pairs.append(before)
        weights.append(pairs)
    for layer in range(2):
        attention, down_full = both_parts(weights[layer][0])
        gate_full, up_full = both_parts(weights[layer][1])
        weights[layer] = (
            attention[:, :qkv],
            attention[:, qkv:],
            (gate_full, up_full),
            down_full.reshape(-1, width),
        )

    segment_ids = lax.dynamic_index_in_dim(segments[:, 0], section, 0, keepdims=False)
    activation = lax.dynamic_index_in_dim(inputs[:, 0], section, 0, keepdims=False).astype(F32)
    upstream = lax.dynamic_index_in_dim(cotangent[:, 0], section, 0, keepdims=False).astype(F32)
    own_ids = lax.dynamic_slice_in_dim(segment_ids, me * rows, rows, 0)
    start = jnp.sum((segment_ids[:, None] < own_ids[None, :]).astype(jnp.int32), 0)
    places = jnp.arange(rows, dtype=jnp.int32)
    pos = me * rows + places
    key_pos = jnp.concatenate([(me ^ d) * rows + places for d in range(fsdp)])
    marks = (start[None, :], pos[None, :], key_pos[:, None])
    freqs = jnp.power(ROPE_BASE, -(jnp.arange(HD // 2, dtype=F32) * 2.0) / HD)
    angle = freqs[:, None] * (pos - start).astype(F32)[None, :]
    cos, sin = jnp.cos(angle), jnp.sin(angle)

    result, kept0 = layer_forward(activation, weights[0], gains[0], cos, sin, marks)
    handed = result.astype(BF16)
    result, kept1 = layer_forward(handed.astype(F32), weights[1], gains[1], cos, sin, marks)
    final = result.astype(BF16)

    def sorted_out(first, second, send_first, send_second):
        received = exchange(jnp.where(on_first, send_second, send_first), "section", 1)
        received = received.astype(first.dtype)
        both = [jnp.where(on_first, first, received), jnp.where(on_first, received, second)]
        return jnp.stack(both)[None, :, None]

    section_output = sorted_out(handed, final, handed, final)

    def heads_back(middle_grad, kept, layer):
        branch = middle_grad.astype(BF16)
        output_grad = dot(kept[5], branch, (1, 0)).astype(BF16)
        heads = dot(weights[layer][1], branch, (1, 1)).astype(BF16).reshape(QH, HD, rows)
        return heads, output_grad

    def second_chunk(qkv_grad, output_grad, down_grad):
        return sum_section(
            jnp.concatenate([qkv_grad, output_grad], 1),
            down_grad.reshape(qkv_grad.shape[0], half),
            on_first,
        )

    middle_grad, gate_grad, up_grad, down_grad, feed_gain1 = feedforward_back(
        upstream, kept1, weights[1], gains[1]
    )
    heads, output_grad = heads_back(middle_grad, kept1, 1)
    early1 = sum_section(gate_grad, up_grad, on_first)
    dq, dk, dv = attend_back(kept1[2], kept1[3], marks, kept1[4], heads)
    dq, dk, dv, early1 = tie(dq, dk, dv, early1)
    grad, qkv_grad, attention_gain1 = projections_back(
        middle_grad, dq, dk, dv, kept1, weights[1], gains[1], cos, sin
    )
    early1 = sum_scatter(early1, "fsdp", 0)
    returned = grad.astype(BF16)
    late1 = second_chunk(qkv_grad, output_grad, down_grad)

    middle_grad, gate_grad, up_grad, down_grad, feed_gain0 = feedforward_back(
        returned.astype(F32), kept0, weights[0], gains[0]
    )
    heads, output_grad = heads_back(middle_grad, kept0, 0)
    heads, early1, late1 = tie(heads, early1, late1)
    early1 = sum_scatter(early1, "rep", 1)
    late1 = sum_scatter(late1, "fsdp", 0)
    early0 = sum_section(gate_grad, up_grad, on_first)
    dq, dk, dv = attend_back(kept0[2], kept0[3], marks, kept0[4], heads)
    dq, dk, dv, early0, early1 = tie(dq, dk, dv, early0, early1)
    early1 = collect(early1, "rep", 1)
    grad, qkv_grad, attention_gain0 = projections_back(
        middle_grad, dq, dk, dv, kept0, weights[0], gains[0], cos, sin
    )
    grad, late1, early1 = tie(grad, late1, early1)
    early0 = sum_scatter(early0, "fsdp", 0)
    late0 = second_chunk(qkv_grad, output_grad, down_grad)
    input_grad = sorted_out(grad, returned.astype(F32), grad.astype(BF16), returned)

    def gathered(part):
        return collect(sum_scatter(part, "rep", 1), "rep", 1)

    def owned(part0, part1):
        other = exchange(jnp.where(on_first, part1, part0), "section", 1)
        left = jnp.where(on_first, part0, other).astype(F32)
        return left, jnp.where(on_first, other, part1).astype(F32)

    late1 = gathered(late1)
    early0 = gathered(early0)
    late0 = gathered(sum_scatter(late0, "fsdp", 0))
    gate_sum, up_sum = owned(early0, early1)
    rest, down_sum = owned(late0, late1)

    gain_grads = jnp.stack([attention_gain0, feed_gain0, attention_gain1, feed_gain1])
    kept = jnp.where(on_first, gain_grads[:2], gain_grads[2:])
    sent = jnp.where(on_first, gain_grads[2:], gain_grads[:2])
    gain_grads = kept + exchange(sent, "section", 1)
    total = gain_grads
    gain_sum = lax.dynamic_slice_in_dim(total, me * depth, depth, 1)
    for d in range(1, fsdp):
        piece = lax.dynamic_slice_in_dim(total, (me ^ d) * depth, depth, 1)
        gain_sum = gain_sum + exchange(piece, "fsdp", d)
    total = gain_sum
    for d in range(1, rep):
        gain_sum = gain_sum + exchange(total, "rep", d)
    return (
        section_output,
        input_grad,
        rest[None, :, :QD],
        rest[None, :, QD : QD + KD],
        rest[None, :, QD + KD : qkv],
        rest[None, :, qkv:],
        gate_sum[None],
        up_sum[None],
        down_sum.reshape(1, -1, width),
        gain_sum[:1],
        gain_sum[1:],
    )


def solution(mesh):
    rows = P("section", "fsdp", None)
    tokens = P("section", None, "rep", "fsdp", None)
    vector = P("section", "fsdp")
    return jax.shard_map(
        body,
        mesh=mesh,
        in_specs=(P(None, "rep", "fsdp", None),) * 2
        + (P(None, "rep", None),)
        + (rows,) * 7
        + (vector,) * 2,
        out_specs=(tokens,) * 2 + (rows,) * 7 + (vector,) * 2,
        check_vma=False,
    )
```

```python
import jax
import jax.numpy as jnp
from jax import lax
from jax.experimental import pallas as pl
from jax.experimental.pallas import tpu as pltpu
from jax.sharding import PartitionSpec as P

QH = 9
KVH = 3
HD = 64
QD = QH * HD
KD = KVH * HD
GROUP = QH // KVH
EPS_NORM = 1e-05
ROPE_BASE = 100000.0
F32 = jnp.float32
BF16 = jnp.bfloat16


def dot(left, right, dims):
    return lax.dot_general(left, right, ((dims[:1], dims[1:]), ((), ())), preferred_element_type=F32)


def exchange(block, axis, distance):
    size = lax.axis_size(axis)
    return lax.ppermute(block, axis, [(i, i ^ distance) for i in range(size)])


def norm_rows(values, gain):
    return values * lax.rsqrt(jnp.mean(values * values, -1, keepdims=True) + EPS_NORM) * gain


def norm_back(values, gain, grad):
    scale = lax.rsqrt(jnp.mean(values * values, -1, keepdims=True) + EPS_NORM)
    unit = values * scale
    pulled = grad * gain
    back = scale * (pulled - unit * jnp.mean(pulled * unit, -1, keepdims=True))
    return back, jnp.sum(grad * unit, 0)


def rope(heads, cos, sin):
    half = HD // 2
    front, back = heads[:, :half], heads[:, half:]
    return jnp.concatenate([front * cos - back * sin, back * cos + front * sin], 1)


def allowed_keys(start_ref, pos_ref, kpos_ref):
    kpos = kpos_ref[...]
    return (kpos >= start_ref[...]) & (kpos <= pos_ref[...])


def attend_kernel(q_ref, k_ref, v_ref, start_ref, pos_ref, kpos_ref, o_ref, lse_ref):
    scores = dot(k_ref[0], q_ref[0], (0, 0))
    scores = jnp.where(allowed_keys(start_ref, pos_ref, kpos_ref), scores, -1e30)
    highest = jnp.max(scores, 0, keepdims=True)
    raised = jnp.exp(scores - highest)
    totals = jnp.sum(raised, 0, keepdims=True)
    weights = (raised * (1.0 / totals)).astype(BF16)
    o_ref[0] = dot(v_ref[0], weights, (1, 0)).astype(BF16)
    lse_ref[0] = highest + jnp.log(totals)


def attend_back_kernel(
    q_ref, k_ref, v_ref, start_ref, pos_ref, kpos_ref, lse_ref, do_ref, dq_ref, dk_ref, dv_ref
):
    query, key, grad_out = q_ref[0], k_ref[0], do_ref[0]
    scores = dot(key, query, (0, 0))
    scores = jnp.where(allowed_keys(start_ref, pos_ref, kpos_ref), scores, -1e30)
    weights = jnp.exp(scores - lse_ref[0])
    grad_weights = dot(v_ref[0], grad_out, (0, 0))
    row = jnp.sum(weights * grad_weights, 0, keepdims=True)
    grad_scores = (weights * (grad_weights - row)).astype(BF16)
    dq_ref[0] = dot(key, grad_scores, (1, 0)) * (HD**-0.5)
    grad_key = dot(query, grad_scores, (1, 1))
    grad_value = dot(grad_out, weights.astype(BF16), (1, 1))
    first = pl.program_id(0) % GROUP == 0

    @pl.when(first)
    def _():
        dk_ref[0] = grad_key
        dv_ref[0] = grad_value

    @pl.when(jnp.logical_not(first))
    def _():
        dk_ref[0] += grad_key
        dv_ref[0] += grad_value


def head_spec(rows, columns, index):
    return pl.BlockSpec((1, rows, columns), index)


def whole_spec(array):
    return pl.BlockSpec(array.shape, lambda h: (0,) * array.ndim)


def attention_specs(queries, keys_values, marks):
    rows, length = queries.shape[2], keys_values.shape[2]
    return [
        head_spec(HD, rows, lambda h: (h, 0, 0)),
        head_spec(HD, length, lambda h: (h // GROUP, 0, 0)),
        head_spec(HD, length, lambda h: (KVH + h // GROUP, 0, 0)),
    ] + [whole_spec(mark) for mark in marks]


PARAMS = pltpu.CompilerParams(vmem_limit_bytes=48 * 1024 * 1024)


def attend(queries, keys_values, marks):
    rows, length = queries.shape[2], keys_values.shape[2]
    return pl.pallas_call(
        attend_kernel,
        grid=(QH,),
        in_specs=attention_specs(queries, keys_values, marks),
        out_specs=[
            head_spec(HD, rows, lambda h: (h, 0, 0)),
            head_spec(1, rows, lambda h: (h, 0, 0)),
        ],
        out_shape=[
            jax.ShapeDtypeStruct((QH, HD, rows), BF16),
            jax.ShapeDtypeStruct((QH, 1, rows), F32),
        ],
        compiler_params=PARAMS,
        cost_estimate=pl.CostEstimate(
            flops=4 * QD * rows * length, bytes_accessed=2 * 2**20, transcendentals=QH * rows * length
        ),
        name="attend",
    )(queries, keys_values, keys_values, *marks)


def attend_back(queries, keys_values, marks, lse, grad_out):
    rows, length = queries.shape[2], keys_values.shape[2]
    return pl.pallas_call(
        attend_back_kernel,
        grid=(QH,),
        in_specs=attention_specs(queries, keys_values, marks)
        + [
            head_spec(1, rows, lambda h: (h, 0, 0)),
            head_spec(HD, rows, lambda h: (h, 0, 0)),
        ],
        out_specs=[
            head_spec(HD, rows, lambda h: (h, 0, 0)),
            head_spec(HD, length, lambda h: (h // GROUP, 0, 0)),
            head_spec(HD, length, lambda h: (h // GROUP, 0, 0)),
        ],
        out_shape=[
            jax.ShapeDtypeStruct((QH, HD, rows), F32),
            jax.ShapeDtypeStruct((KVH, HD, length), F32),
            jax.ShapeDtypeStruct((KVH, HD, length), F32),
        ],
        compiler_params=PARAMS,
        cost_estimate=pl.CostEstimate(
            flops=10 * QD * rows * length, bytes_accessed=4 * 2**20, transcendentals=QH * rows * length
        ),
        name="attend_back",
    )(queries, keys_values, keys_values, *marks, lse, grad_out)


def layer_forward(activation, weights, gains, cos, sin, marks, at_keys, at_attended):
    qkv_weight, output_weight, down_weight = weights
    rows = activation.shape[0]
    fsdp = lax.axis_size("fsdp")
    normed = norm_rows(activation, gains[0]).astype(BF16)
    heads = dot(qkv_weight, normed, (0, 1)).reshape(QH + 2 * KVH, HD, rows)
    queries = (rope(heads[:QH], cos, sin).astype(BF16) * (HD**-0.5)).astype(BF16)
    mine = jnp.concatenate(
        [rope(heads[QH : QH + KVH], cos, sin).astype(BF16), heads[QH + KVH :].astype(BF16)], 0
    )
    keys_values = jnp.concatenate(
        [mine] + [exchange(mine, "fsdp", d) for d in range(1, fsdp)], 2
    )
    keys_values = at_keys(keys_values)
    attended, lse = attend(queries, keys_values, marks)
    attended, gate_up = at_attended(attended.reshape(QD, rows))
    middle = activation + dot(attended, output_weight, (0, 0))
    normed_mid = norm_rows(middle, gains[1]).astype(BF16)
    gate, lift = [dot(normed_mid, weight, (1, 0)) for weight in gate_up]
    hidden = (gate * jax.nn.sigmoid(gate) * lift).astype(BF16)
    result = middle + dot(hidden, down_weight, (1, 0))
    weights = (qkv_weight, output_weight, gate_up, down_weight)
    kept = (activation, normed, queries, keys_values, lse, attended, middle, normed_mid, gate, lift, hidden)
    return result, kept, weights


def feedforward_back(grad, kept, weights, gains):
    _, _, gate_up, down_weight = weights
    middle, normed_mid, gate, lift, hidden = kept[6:]
    branch = grad.astype(BF16)
    down_grad = dot(hidden, branch, (0, 0)).astype(BF16)
    hidden_grad = dot(branch, down_weight, (1, 1))
    sigma = jax.nn.sigmoid(gate)
    gate_part = (hidden_grad * lift * sigma * (1.0 + gate * (1.0 - sigma))).astype(BF16)
    lift_part = (hidden_grad * gate * sigma).astype(BF16)
    gate_grad = dot(normed_mid, gate_part, (0, 0)).astype(BF16)
    up_grad = dot(normed_mid, lift_part, (0, 0)).astype(BF16)
    pulled = dot(gate_part, gate_up[0], (1, 1)) + dot(lift_part, gate_up[1], (1, 1))
    back, gain_grad = norm_back(middle, gains[1], pulled)
    return grad + back, gate_grad, up_grad, down_grad, gain_grad


def projections_back(middle_grad, dq, dk, dv, kept, weights, gains, cos, sin):
    activation, normed = kept[:2]
    qkv_weight = weights[0]
    rows = activation.shape[0]
    fsdp = lax.axis_size("fsdp")
    parts = jnp.concatenate([dk, dv], 0).astype(BF16)
    pieces = [parts[:, :, d * rows : (d + 1) * rows] for d in range(fsdp)]
    summed = pieces[0].astype(F32)
    for d in range(1, fsdp):
        summed = summed + exchange(pieces[d], "fsdp", d).astype(F32)
    turned = rope(jnp.concatenate([dq, summed[:KVH]], 0), cos, -sin)
    raw = jnp.concatenate([turned, summed[KVH:]], 0).astype(BF16).reshape(QD + 2 * KD, rows)
    qkv_grad = dot(normed, raw, (0, 1)).astype(BF16)
    back, gain_grad = norm_back(activation, gains[0], dot(raw, qkv_weight, (0, 1)))
    return middle_grad + back, qkv_grad, gain_grad


def sum_section(left, right, on_first):
    other = exchange(jnp.where(on_first, right, left), "section", 1)
    return (jnp.where(on_first, left, right).astype(F32) + other.astype(F32)).astype(BF16)


def sum_scatter(total, axis, dim):
    size, me = lax.axis_size(axis), lax.axis_index(axis)
    span = total.shape[dim] // size
    own = lax.dynamic_slice_in_dim(total, me * span, span, dim).astype(F32)
    for d in range(1, size):
        piece = lax.dynamic_slice_in_dim(total, (me ^ d) * span, span, dim)
        own = own + exchange(piece, axis, d).astype(F32)
    return own.astype(BF16)


def fetch(share, axis):
    return [share] + [exchange(share, axis, d) for d in range(1, lax.axis_size(axis))]


def place(blocks, axis, dim):
    me = lax.axis_index(axis)
    span = blocks[0].shape[dim]
    shape = list(blocks[0].shape)
    shape[dim] = span * len(blocks)
    full = jnp.zeros(shape, blocks[0].dtype)
    for d, block in enumerate(blocks):
        full = lax.dynamic_update_slice_in_dim(full, block, (me ^ d) * span, dim)
    return full


def collect(share, axis, dim):
    return place(fetch(share, axis), axis, dim)


def tie(*arrays):
    return lax.optimization_barrier(arrays)


def body(inputs, cotangent, segments, *shards):
    query, key, value, output, gate, up, down = [shard[0] for shard in shards[:7]]
    section = lax.axis_index("section")
    on_first = section == 0
    fsdp, rep = lax.axis_size("fsdp"), lax.axis_size("rep")
    me = lax.axis_index("fsdp")
    rows, width = inputs.shape[2], inputs.shape[3]
    depth, half = gate.shape
    qkv = QD + 2 * KD

    attention_shard = jnp.concatenate([query, key, value, output], 1)
    down_shard = down.reshape(depth, half)
    shares = []
    for left, right in ((attention_shard, down_shard), (gate, up)):
        swapped = exchange(jnp.where(on_first, right, left), "section", 1)
        shares.append(
            (jnp.where(on_first, left, swapped), jnp.where(on_first, swapped, right))
        )
    gain_shard = jnp.concatenate(shards[7:9], 0)
    other = exchange(gain_shard, "section", 1)
    gain_shard = jnp.stack(
        [jnp.where(on_first, gain_shard, other), jnp.where(on_first, other, gain_shard)]
    )
    gains = collect(gain_shard[None], "fsdp", 0)
    gains = jnp.transpose(gains, (1, 2, 0, 3)).reshape(2, 2, width).astype(F32)

    def both_parts(full):
        other = exchange(full, "section", 1)
        return jnp.where(on_first, full, other), jnp.where(on_first, other, full)

    def attention_part(blocks):
        attention, down_full = both_parts(place(blocks, "fsdp", 0))
        return attention[:, :qkv], attention[:, qkv:], down_full.reshape(-1, width)

    pending = {"attention0": fetch(shares[0][0], "fsdp")}
    share, *blocks = tie(shares[1][0], *pending["attention0"])
    pending["feed0"] = fetch(share, "fsdp")

    def keys_here(keys_values):
        keys_values, share = tie(keys_values, shares[0][1])
        pending["attention1"] = fetch(share, "fsdp")
        return keys_values

    def attended_here(layer):
        def hook(attended):
            attended, share, *arrived = tie(attended, shares[1][1], *pending["feed%d" % layer])
            if layer == 0:
                pending["feed1"] = fetch(share, "fsdp")
            return attended, both_parts(place(arrived, "fsdp", 0))

        return hook

    segment_ids = lax.dynamic_index_in_dim(segments[:, 0], section, 0, keepdims=False)
    activation = lax.dynamic_index_in_dim(inputs[:, 0], section, 0, keepdims=False).astype(F32)
    upstream = lax.dynamic_index_in_dim(cotangent[:, 0], section, 0, keepdims=False).astype(F32)
    own_ids = lax.dynamic_slice_in_dim(segment_ids, me * rows, rows, 0)
    start = jnp.sum((segment_ids[:, None] < own_ids[None, :]).astype(jnp.int32), 0)
    places = jnp.arange(rows, dtype=jnp.int32)
    pos = me * rows + places
    key_pos = jnp.concatenate([(me ^ d) * rows + places for d in range(fsdp)])
    marks = (start[None, :], pos[None, :], key_pos[:, None])
    freqs = jnp.power(ROPE_BASE, -(jnp.arange(HD // 2, dtype=F32) * 2.0) / HD)
    angle = freqs[:, None] * (pos - start).astype(F32)[None, :]
    cos, sin = jnp.cos(angle), jnp.sin(angle)

    result, kept0, weights0 = layer_forward(
        activation, attention_part(blocks), gains[0], cos, sin, marks, keys_here, attended_here(0)
    )
    handed, *blocks = tie(result.astype(BF16), *pending["attention1"])
    result, kept1, weights1 = layer_forward(
        handed.astype(F32),
        attention_part(blocks),
        gains[1],
        cos,
        sin,
        marks,
        lambda keys_values: keys_values,
        attended_here(1),
    )
    weights = (weights0, weights1)
    final = result.astype(BF16)

    def sorted_out(first, second, send_first, send_second):
        received = exchange(jnp.where(on_first, send_second, send_first), "section", 1)
        received = received.astype(first.dtype)
        both = [jnp.where(on_first, first, received), jnp.where(on_first, received, second)]
        return jnp.stack(both)[None, :, None]

    section_output = sorted_out(handed, final, handed, final)

    def heads_back(middle_grad, kept, layer):
        branch = middle_grad.astype(BF16)
        output_grad = dot(kept[5], branch, (1, 0)).astype(BF16)
        heads = dot(weights[layer][1], branch, (1, 1)).astype(BF16).reshape(QH, HD, rows)
        return heads, output_grad

    def second_chunk(qkv_grad, output_grad, down_grad):
        return sum_section(
            jnp.concatenate([qkv_grad, output_grad], 1),
            down_grad.reshape(qkv_grad.shape[0], half),
            on_first,
        )

    middle_grad, gate_grad, up_grad, down_grad, feed_gain1 = feedforward_back(
        upstream, kept1, weights[1], gains[1]
    )
    heads, output_grad = heads_back(middle_grad, kept1, 1)
    early1 = sum_section(gate_grad, up_grad, on_first)
    dq, dk, dv = attend_back(kept1[2], kept1[3], marks, kept1[4], heads)
    dq, dk, dv, early1 = tie(dq, dk, dv, early1)
    grad, qkv_grad, attention_gain1 = projections_back(
        middle_grad, dq, dk, dv, kept1, weights[1], gains[1], cos, sin
    )
    early1 = sum_scatter(early1, "fsdp", 0)
    returned = grad.astype(BF16)
    late1 = second_chunk(qkv_grad, output_grad, down_grad)

    middle_grad, gate_grad, up_grad, down_grad, feed_gain0 = feedforward_back(
        returned.astype(F32), kept0, weights[0], gains[0]
    )
    heads, output_grad = heads_back(middle_grad, kept0, 0)
    early0 = sum_section(gate_grad, up_grad, on_first)
    heads, early1, late1, early0 = tie(heads, early1, late1, early0)
    early1 = sum_scatter(early1, "rep", 1)
    late1 = sum_scatter(late1, "fsdp", 0)
    dq, dk, dv = attend_back(kept0[2], kept0[3], marks, kept0[4], heads)
    dq, dk, dv, early1 = tie(dq, dk, dv, early1)
    early0 = sum_scatter(early0, "fsdp", 0)
    early1 = collect(early1, "rep", 1)
    grad, qkv_grad, attention_gain0 = projections_back(
        middle_grad, dq, dk, dv, kept0, weights[0], gains[0], cos, sin
    )
    grad, late1, early1, early0 = tie(grad, late1, early1, early0)
    late0 = second_chunk(qkv_grad, output_grad, down_grad)
    input_grad = sorted_out(grad, returned.astype(F32), grad.astype(BF16), returned)

    def owned(part0, part1):
        other = exchange(jnp.where(on_first, part1, part0), "section", 1)
        left = jnp.where(on_first, part0, other).astype(F32)
        return left, jnp.where(on_first, other, part1).astype(F32)

    late1, early0, late0 = tie(late1, early0, late0)
    late1, early0 = sum_scatter(late1, "rep", 1), sum_scatter(early0, "rep", 1)
    late1, early0, late0 = tie(late1, early0, sum_scatter(late0, "fsdp", 0))
    late1, early0 = collect(late1, "rep", 1), collect(early0, "rep", 1)
    late0 = collect(sum_scatter(late0, "rep", 1), "rep", 1)
    gate_sum, up_sum = owned(early0, early1)
    rest, down_sum = owned(late0, late1)

    gain_grads = jnp.stack([attention_gain0, feed_gain0, attention_gain1, feed_gain1])
    kept = jnp.where(on_first, gain_grads[:2], gain_grads[2:])
    sent = jnp.where(on_first, gain_grads[2:], gain_grads[:2])
    gain_grads = kept + exchange(sent, "section", 1)
    total = gain_grads
    gain_sum = lax.dynamic_slice_in_dim(total, me * depth, depth, 1)
    for d in range(1, fsdp):
        piece = lax.dynamic_slice_in_dim(total, (me ^ d) * depth, depth, 1)
        gain_sum = gain_sum + exchange(piece, "fsdp", d)
    total = gain_sum
    for d in range(1, rep):
        gain_sum = gain_sum + exchange(total, "rep", d)
    return (
        section_output,
        input_grad,
        rest[None, :, :QD],
        rest[None, :, QD : QD + KD],
        rest[None, :, QD + KD : qkv],
        rest[None, :, qkv:],
        gate_sum[None],
        up_sum[None],
        down_sum.reshape(1, -1, width),
        gain_sum[:1],
        gain_sum[1:],
    )


def solution(mesh):
    rows = P("section", "fsdp", None)
    tokens = P("section", None, "rep", "fsdp", None)
    vector = P("section", "fsdp")
    return jax.shard_map(
        body,
        mesh=mesh,
        in_specs=(P(None, "rep", "fsdp", None),) * 2
        + (P(None, "rep", None),)
        + (rows,) * 7
        + (vector,) * 2,
        out_specs=(tokens,) * 2 + (rows,) * 7 + (vector,) * 2,
        check_vma=False,
    )
```
